32 devices in a mesh: head: 2 (over y), tok: 16 (over z, x, core).
Axes of the slice: x: 2, y: 2, z: 4, core: 2. Of those that a mesh axis runs over, the one named last changes fastest.
Arguments:
- queries: bfloat16 [2, 16, 4096, 256], P(None, 'head', 'tok'), may hold values from -6 to 6
- key_vectors: bfloat16 [2, 16, 4096, 256], P(None, 'head', 'tok'), may hold values from -6 to 6
- value_vectors: bfloat16 [2, 16, 4096, 256], P(None, 'head', 'tok'), may hold values from -6 to 6
- step_rates: bfloat16 [2, 16, 4096], P(None, 'head', 'tok'), may hold values from 0.029907227 to 0.29882812
- counts: int32 [2, 16], replicated, may hold values from 1 to 256, 2560 in all within a row
- out_gain: float32 [16, 256], P('head'), may hold values from 0.25 to 1.75
- w_gate: float32 [16, 512, 256], P('head', 'tok'), may hold values from -0.375 to 0.375
- w_up: float32 [16, 512, 256], P('head', 'tok'), may hold values from -0.375 to 0.375
- w_down: float32 [16, 256, 512], P('head', 'tok'), may hold values from -0.25 to 0.25
Outputs:
- mixed_out: bfloat16 [2, 16, 4096, 256], P(None, 'head', 'tok')
- final_gate: float32 [16, 512, 256], P('head', 'tok')
- final_up: float32 [16, 512, 256], P('head', 'tok')
- final_down: float32 [16, 256, 512], P('head', 'tok')
The draws below stay inside these ranges and needn't reach their ends.
Inputs may be any that keep to these rules, and one draw needn't show every extreme that they name: `counts`: the valid tokens are the first ones of each block of 256; each row sums to 256 * 16 * 5 // 8 and some block of each group is full.
All inputs are finite; a program needn't handle non-finite values.
Results may differ from the reference program's by a relative error of at most 0.011.
Values may be sent and summed in bfloat16 or wider, within the bound.
A program may use at most 128 MiB of HBM per device.

```python
import math
import jax
import jax.numpy as jnp
import numpy as np
from jax import lax

HEADS = 16
DH = 256
FH = 512
BLK = 256
GROUPS = 2
TOKENS = 4096
N_TOK = 16


def level_of(stream_key, dims, split, low, top_value):
    def one(dim, parts):
        heights = jax.random.uniform(jax.random.fold_in(jax.random.fold_in(stream_key, 6), dim), (parts,), jnp.float32, low / len(split), top_value / len(split))
        return jnp.repeat(jnp.exp(heights), dims[dim] // parts).reshape((-1,) + (1,) * (len(dims) - dim - 1))

    gain = one(*split[0])
    for cut in split[1:]:
        gain = gain * one(*cut)
    return gain


def profile(count, total, limit, skew):
    loads = [(1 << 20) // math.isqrt(standing ** skew) + 1 for standing in range(2, count + 1)]
    spare, given = total - limit - (count - 1), [1] * (count - 1)
    while spare > 0:
        movable = [i for i in range(count - 1) if given[i] < limit]
        pool, left = sum([loads[i] for i in movable]), spare
        for i in movable:
            extra = min(limit - given[i], max(1, left * loads[i] // pool), spare)
            given[i] = given[i] + extra
            spare = spare - extra
    return np.array([limit] + given)


def ragged_sizes(key, count, total, bound, lean):
    if count == 2:
        one = jax.random.randint(key, (), max(1, total - bound), min(bound, total - 1) + 1)
        return jnp.stack([one, total - one])
    sizes = jnp.asarray(profile(count, total, bound, lean), jnp.int32)
    twos = (count - 1) // 2
    source_of, sink = sizes[1:1 + 2 * twos:2], sizes[2:2 + 2 * twos:2]
    slack = jnp.minimum(source_of - 1, bound - sink)
    passed = jax.random.randint(jax.random.fold_in(key, 1), (twos,), 0, 1 << 20) % (slack + 1)
    sizes = sizes.at[1:1 + 2 * twos:2].set(source_of - passed).at[2:2 + 2 * twos:2].set(sink + passed)
    return sizes[jax.random.permutation(jax.random.fold_in(key, 2), count)]


def gaussian(own_key, extent, spread, most, cuts=(), kind=jnp.bfloat16):
    array = spread * jax.random.normal(own_key, extent, jnp.float32)
    if cuts:
        array = array * level_of(own_key, extent, cuts, -0.22, 0.18)
    return jnp.clip(array, -most, most).astype(kind)


def setup_inputs(seed: int = 0) -> dict:
    keys = jax.random.split(jax.random.key(seed), 10)
    return {
        "queries": gaussian(keys[0], (GROUPS, HEADS, TOKENS, DH), 1.0, 6.0, ((1, 2), (2, 16))),
        "key_vectors": gaussian(keys[1], (GROUPS, HEADS, TOKENS, DH), 1.0, 6.0, ((1, 2), (2, 16))),
        "value_vectors": gaussian(keys[2], (GROUPS, HEADS, TOKENS, DH), 1.0, 6.0, ((1, 2), (2, 16))),
        "step_rates": jnp.clip(jnp.exp(math.log(0.29882812) - 2.30176843 * jax.random.uniform(keys[3], (GROUPS, HEADS, TOKENS), jnp.float32) ** level_of(keys[3], (GROUPS, HEADS, TOKENS), ((1, 2), (2, 16)), -0.2, 0.2)), 0.029907227, 0.29882812).astype(jnp.bfloat16),
        "counts": jax.vmap(lambda own: ragged_sizes(own, N_TOK, BLK * N_TOK * 5 // 8, BLK, 2))(jax.random.split(keys[4], GROUPS)).reshape((GROUPS, N_TOK)).astype(jnp.int32),
        "out_gain": jnp.clip(1.0 + 0.15 * jax.random.normal(keys[5], (HEADS, DH), jnp.float32), 0.25, 1.75),
        "w_gate": gaussian(keys[6], (HEADS, FH, DH), DH ** -0.5, 0.375, ((0, 2), (1, 16)), jnp.float32),
        "w_up": gaussian(keys[7], (HEADS, FH, DH), DH ** -0.5, 0.375, ((0, 2), (1, 16)), jnp.float32),
        "w_down": gaussian(keys[8], (HEADS, DH, FH), FH ** -0.5, 0.25, ((0, 2), (1, 16)), jnp.float32),
    }


epsilon = 1e-06

def renorm(previous, stepped):
    kept_norm = jnp.sqrt(lax.optimization_barrier(jnp.mean(previous * previous, axis=-1, keepdims=True)))
    return stepped * kept_norm * lax.rsqrt(lax.optimization_barrier(jnp.mean(stepped * stepped, axis=-1, keepdims=True)) + epsilon)

def reference(queries, key_vectors, value_vectors, step_rates, counts, out_gain, w_gate, w_up, w_down):
    grad_scale = float(TOKENS) ** (-0.5)
    positions = jnp.arange(TOKENS, dtype=jnp.int32)
    masters = (w_gate, w_up, w_down)
    outputs = []
    for group in range(GROUPS):
        limits = jnp.take(counts[group], positions // BLK)
        valid_mask = (positions % BLK < limits).astype(jnp.float32)
        fast = tuple((weight_set.astype(jnp.bfloat16) for weight_set in masters))

        def update_head(items):
            gate_w, up_w, down_w, key_rows, value_rows, rate_rows = items
            gate_pre = jnp.dot(key_rows, gate_w.T, preferred_element_type=jnp.float32)
            up_pre = jnp.dot(key_rows, up_w.T, preferred_element_type=jnp.float32)
            sigmoid_gate = jax.nn.sigmoid(gate_pre)
            activated = gate_pre * sigmoid_gate
            hidden = (activated * up_pre).astype(jnp.bfloat16)
            weighted = (value_rows.astype(jnp.float32) * (rate_rows.astype(jnp.float32) * grad_scale * valid_mask)[:, None]).astype(jnp.bfloat16)
            back = jnp.dot(weighted, down_w, preferred_element_type=jnp.float32)
            grad_gate = (back * up_pre * sigmoid_gate * (1.0 + gate_pre * (1.0 - sigmoid_gate))).astype(jnp.bfloat16)
            grad_up = (back * activated).astype(jnp.bfloat16)
            upd_gate = jnp.dot(grad_gate.T, key_rows, preferred_element_type=jnp.float32)
            upd_up = jnp.dot(grad_up.T, key_rows, preferred_element_type=jnp.float32)
            upd_down = jnp.dot(weighted.T, hidden, preferred_element_type=jnp.float32)
            return (upd_gate, upd_up, upd_down)
        updates = lax.map(update_head, (fast[0], fast[1], fast[2], key_vectors[group], value_vectors[group], step_rates[group]))
        masters = tuple((renorm(previous, previous + update) for previous, update in zip(masters, updates)))
        fast = tuple((weight_set.astype(jnp.bfloat16) for weight_set in masters))

        def apply_head(items):
            gate_w, up_w, down_w, query_rows = items
            gate_pre = jnp.dot(query_rows, gate_w.T, preferred_element_type=jnp.float32)
            up_pre = jnp.dot(query_rows, up_w.T, preferred_element_type=jnp.float32)
            hidden = (gate_pre * jax.nn.sigmoid(gate_pre) * up_pre).astype(jnp.bfloat16)
            return jnp.dot(hidden, down_w.T, preferred_element_type=jnp.float32) * valid_mask[:, None]
        heads_out = lax.map(apply_head, (fast[0], fast[1], fast[2], queries[group]))
        mean_square = lax.optimization_barrier(jnp.sum(heads_out * heads_out, axis=(0, 2))) / (HEADS * DH)
        normed = (heads_out * out_gain[:, None, :] * lax.rsqrt(mean_square + epsilon)[None, :, None]).astype(jnp.bfloat16)
        outputs.append(normed)
    return (jnp.stack(outputs), masters[0], masters[1], masters[2])
```

```python
import functools

import jax
import jax.numpy as jnp
from jax import lax
from jax.experimental import pallas as pl
from jax.experimental.pallas import tpu as pltpu
from jax.sharding import PartitionSpec as P

epsilon = 1e-06
MESH = pl.DeviceIdType.MESH
NT = (((1,), (1,)), ((), ()))


def dot_nt(left, right):
    return lax.dot_general(left, right, NT, preferred_element_type=jnp.float32)


def dot_nn(left, right):
    return jnp.dot(left, right, preferred_element_type=jnp.float32)


def sigmoid(x):
    return 0.5 * jnp.tanh(0.5 * x) + 0.5


def renorm(previous, stepped):
    kept = jnp.sqrt(jnp.mean(previous * previous, axis=-1, keepdims=True))
    return (
        stepped
        * kept
        * lax.rsqrt(jnp.mean(stepped * stepped, axis=-1, keepdims=True) + epsilon)
    )


def kernel(
    dims,
    k_ref, e_ref, q_ref, mask_ref, gain_ref, wg_ref, wu_ref, wd_ref,
    out_ref, fg_ref, fu_ref, fd_ref,
    kbuf, ebuf, qbuf, o_send, o_recv,
    gu_m, d_m, gu_b, d_b, dt_b,
    dgu, ddt, dd,
    rs_send, rs_recv, rsd_send, rsd_recv,
    ms_send, ms_recv,
    tok_s, tok_r, w_s, w_r, o_s, o_r, f_s, f_r,
    rs_s, rs_r, ag_s, ag_r, ms_s, ms_r,
):
    tok_n, head_n, parts, reps, per = dims
    groups = k_ref.shape[0]
    heads = k_ref.shape[1]
    width = k_ref.shape[3]
    hidden = wd_ref.shape[2]
    gate_rows, down_rows = wg_ref.shape[1], wd_ref.shape[1]
    gate_part, down_part = parts * gate_rows, parts * down_rows
    tok = lax.axis_index("tok")
    hid = lax.axis_index("head")
    mine = lax.rem(tok, parts)
    rep = tok // parts

    part_peers = [lax.rem(mine + s, parts) for s in range(1, parts)]
    rep_peers = [lax.rem(rep + s, reps) for s in range(1, reps)]
    head_peers = [lax.rem(hid + s, head_n) for s in range(1, head_n)]

    def part_dev(index):
        return (hid, rep * parts + index)

    def rep_dev(index):
        return (hid, index * parts + mine)

    barrier = pltpu.get_barrier_semaphore()
    everyone = (
        [part_dev(j) for j in part_peers]
        + [rep_dev(j) for j in rep_peers]
        + [(j, tok) for j in head_peers]
    )
    for device in everyone:
        pl.semaphore_signal(barrier, inc=1, device_id=device, device_id_type=MESH)
    pl.semaphore_wait(barrier, len(everyone))

    pending = []

    def remote(src, dst, send, recv, device):
        return pltpu.make_async_remote_copy(
            src_ref=src, dst_ref=dst, send_sem=send, recv_sem=recv,
            device_id=device, device_id_type=MESH,
        )

    def push(src, dst, send, recv, device):
        copy = remote(src, dst, send, recv, device)
        copy.start()
        pending.append(copy)

    def rows_of(index, size):
        return pl.ds(pl.multiple_of(index * size, size), size)

    def heads_of(index):
        return pl.ds(index * per, per)

    tokens = ((k_ref, kbuf), (e_ref, ebuf), (q_ref, qbuf))

    def send_tokens(group, kinds):
        for s, j in enumerate(part_peers):
            for kind in kinds:
                src, dst = tokens[kind]
                push(
                    src.at[group, heads_of(j)], dst.at[group, mine],
                    tok_s.at[group, kind, s], tok_r.at[group, kind, s], part_dev(j),
                )

    def wait_tokens(group, kinds, source, s):
        for kind in kinds:
            dst = tokens[kind][1].at[group, source]
            remote(
                dst, dst, tok_s.at[group, kind, s], tok_r.at[group, kind, s], part_dev(source)
            ).wait_recv()

    weights = (
        (wg_ref, gu_m.at[0], gate_rows), (wu_ref, gu_m.at[1], gate_rows), (wd_ref, d_m, down_rows)
    )
    for s, j in enumerate(part_peers):
        for kind, (src, dst, rows) in enumerate(weights):
            push(
                src.at[heads_of(j)], dst.at[:, rows_of(mine, rows)],
                w_s.at[kind, s], w_r.at[kind, s], part_dev(j),
            )
    send_tokens(0, (0, 1))
    send_tokens(0, (2,))
    for src, dst, rows in weights:
        dst[:, rows_of(mine, rows)] = src[heads_of(mine)]
    for group in range(groups):
        for src, dst in tokens:
            dst[group, mine] = src[group, heads_of(mine)]

    def share(stage):
        gate_own, down_own = rows_of(rep, gate_part), rows_of(rep, down_part)
        gu_b[stage, :, :, gate_own] = gu_m[...].astype(jnp.bfloat16)
        d_b[stage, :, down_own] = d_m[...].astype(jnp.bfloat16)
        for s, j in enumerate(rep_peers):
            gu = gu_b.at[stage, :, :, gate_own]
            push(gu, gu, ag_s.at[stage, 0, s], ag_r.at[stage, 0, s], rep_dev(j))
            down = d_b.at[stage, :, down_own]
            push(down, down, ag_s.at[stage, 1, s], ag_r.at[stage, 1, s], rep_dev(j))

    def wait_share(stage):
        for s in range(reps - 1):
            j = lax.rem(rep + reps - 1 - s, reps)
            gu = gu_b.at[stage, :, :, rows_of(j, gate_part)]
            remote(gu, gu, ag_s.at[stage, 0, s], ag_r.at[stage, 0, s], rep_dev(j)).wait_recv()
            down = d_b.at[stage, :, rows_of(j, down_part)]
            remote(down, down, ag_s.at[stage, 1, s], ag_r.at[stage, 1, s], rep_dev(j)).wait_recv()

    def update(group):
        dgu[...] = jnp.zeros_like(dgu)
        ddt[...] = jnp.zeros_like(ddt)
        for h in range(per):
            dt_b[h] = d_b[group, h].astype(jnp.float32).T.astype(jnp.bfloat16)

        def one(source):
            for h in range(per):
                key = kbuf[group, source, h]
                err = ebuf[group, source, h]
                a = dot_nt(gu_b[group, 0, h], key)
                b = dot_nt(gu_b[group, 1, h], key)
                r = dot_nt(dt_b[h], err)
                sg = sigmoid(a)
                act = a * sg
                ddt[h] += dot_nn((act * b).astype(jnp.bfloat16), err)
                da = (r * b * sg * (1.0 + a * (1.0 - sg))).astype(jnp.bfloat16)
                dgu[0, h] += dot_nn(da, key)
                dgu[1, h] += dot_nn((r * act).astype(jnp.bfloat16), key)

        def step(s, carry):
            source = lax.rem(mine + parts - s, parts)

            @pl.when(s > 0)
            def _():
                wait_tokens(group, (0, 1), source, s - 1)

            one(source)
            return carry

        lax.fori_loop(0, parts, step, 0)
        for h in range(per):
            dd[h] = ddt[h].T

    def scatter(group):
        for s, j in enumerate(rep_peers):
            rs_send[group, s] = dgu[:, :, rows_of(j, gate_part)].astype(jnp.bfloat16)
            push(
                rs_send.at[group, s], rs_recv.at[group, s],
                rs_s.at[group, 0, s], rs_r.at[group, 0, s], rep_dev(j),
            )
            rsd_send[group, s] = dd[:, rows_of(j, down_part)].astype(jnp.bfloat16)
            push(
                rsd_send.at[group, s], rsd_recv.at[group, s],
                rs_s.at[group, 1, s], rs_r.at[group, 1, s], rep_dev(j),
            )

    def settle(group):
        gate = gu_m[...] + dgu[:, :, rows_of(rep, gate_part)]
        down = d_m[...] + dd[:, rows_of(rep, down_part)]
        for s in range(reps - 1):
            j = lax.rem(rep + reps - 1 - s, reps)
            got = rs_recv.at[group, s]
            remote(got, got, rs_s.at[group, 0, s], rs_r.at[group, 0, s], rep_dev(j)).wait_recv()
            gate = gate + got[...].astype(jnp.float32)
            got = rsd_recv.at[group, s]
            remote(got, got, rs_s.at[group, 1, s], rs_r.at[group, 1, s], rep_dev(j)).wait_recv()
            down = down + got[...].astype(jnp.float32)
        gu_m[...] = renorm(gu_m[...], gate)
        d_m[...] = renorm(d_m[...], down)

    def apply(group):
        stage = group + 1

        def one(source, into):
            for h in range(per):
                query = qbuf[group, source, h]
                a = dot_nt(query, gu_b[stage, 0, h])
                b = dot_nt(query, gu_b[stage, 1, h])
                hid_act = (a * sigmoid(a) * b).astype(jnp.bfloat16)
                into[h] = dot_nt(hid_act, d_b[stage, h]).astype(jnp.bfloat16)

        def out_copy(s):
            source = lax.rem(mine + parts - 1 - s, parts)
            return remote(
                o_send.at[group, s], o_recv.at[group, mine],
                o_s.at[group, s], o_r.at[group, s], part_dev(source),
            )

        def step(s, carry):
            source = lax.rem(mine + parts - 1 - s, parts)
            wait_tokens(group, (2,), source, s)
            one(source, o_send.at[group, s])
            out_copy(s).start()
            return carry

        lax.fori_loop(0, parts - 1, step, 0)
        one(mine, o_recv.at[group, mine])
        for s in range(parts - 1):
            pending.append(out_copy(s))

    def finish(group):
        for s, j in enumerate(part_peers):
            got = o_recv.at[group, j]
            remote(got, got, o_s.at[group, s], o_r.at[group, s], part_dev(j)).wait_recv()
        half = width // 2
        total = jnp.zeros((k_ref.shape[2], half), jnp.float32)
        for head in range(heads):
            o = o_recv[group, head // per, head % per].astype(jnp.float32)
            total = total + (o[:, :half] * o[:, :half] + o[:, half:] * o[:, half:])
        ms_send[group] = total
        for s, j in enumerate(head_peers):
            push(
                ms_send.at[group], ms_recv.at[group, s],
                ms_s.at[group, s], ms_r.at[group, s], (j, tok),
            )
        for s in range(head_n - 1):
            j = lax.rem(hid + head_n - 1 - s, head_n)
            got = ms_recv.at[group, s]
            remote(got, got, ms_s.at[group, s], ms_r.at[group, s], (j, tok)).wait_recv()
            total = total + got[...]
        mean = jnp.sum(total, axis=1, keepdims=True) / (head_n * heads * width)
        scale = lax.rsqrt(mean + epsilon) * mask_ref[group]
        for head in range(heads):
            o = o_recv[group, head // per, head % per].astype(jnp.float32)
            out_ref[group, head] = (o * gain_ref[pl.ds(head, 1), :] * scale).astype(jnp.bfloat16)

    for s in range(parts - 1):
        j = lax.rem(mine + parts - 1 - s, parts)
        for kind, (_, dst, rows) in enumerate(weights):
            got = dst.at[:, rows_of(j, rows)]
            remote(got, got, w_s.at[kind, s], w_r.at[kind, s], part_dev(j)).wait_recv()
    share(0)
    wait_share(0)
    for group in range(groups):
        update(group)
        scatter(group)
        if group + 1 < groups:
            send_tokens(group + 1, (0, 1, 2))
        if group > 0:
            apply(group - 1)
        settle(group)
        share(group + 1)
        if group > 0:
            finish(group - 1)
        if group + 1 == groups:
            finals = ((gu_m.at[0], fg_ref, gate_rows), (gu_m.at[1], fu_ref, gate_rows),
                      (d_m, fd_ref, down_rows))
            for s, j in enumerate(part_peers):
                for kind, (src, dst, rows) in enumerate(finals):
                    push(
                        src.at[:, rows_of(j, rows)], dst.at[heads_of(mine)],
                        f_s.at[kind, s], f_r.at[kind, s], part_dev(j),
                    )
            for src, dst, rows in finals:
                dst[heads_of(mine)] = src[:, rows_of(mine, rows)]
        wait_share(group + 1)
    apply(groups - 1)
    finish(groups - 1)
    for s in range(parts - 1):
        j = lax.rem(mine + parts - 1 - s, parts)
        for kind, (_, dst, rows) in enumerate(finals):
            got = dst.at[heads_of(j)]
            remote(got, got, f_s.at[kind, s], f_r.at[kind, s], part_dev(j)).wait_recv()
    for copy in pending:
        copy.wait_send()


def on_device(
    queries, key_vectors, value_vectors, step_rates, counts, out_gain, w_gate, w_up, w_down
):
    tok_n, head_n = lax.axis_size("tok"), lax.axis_size("head")
    groups, heads, block, width = key_vectors.shape
    hidden = w_down.shape[2]
    parts = min(heads, tok_n)
    per, reps = heads // parts, tok_n // parts
    gate_rows, down_rows = w_gate.shape[1], w_down.shape[1]
    gate_part, down_part = parts * gate_rows, parts * down_rows
    grad_scale = float(tok_n * block) ** (-0.5)
    own = lax.dynamic_slice_in_dim(counts, lax.axis_index("tok"), 1, 1)
    mask = (jnp.arange(block, dtype=jnp.int32)[None, :] < own).astype(jnp.float32)
    rate = step_rates.astype(jnp.float32) * grad_scale * mask[:, None, :]
    errors = (value_vectors.astype(jnp.float32) * rate[..., None]).astype(jnp.bfloat16)

    bf16, f32 = jnp.bfloat16, jnp.float32
    vmem, dma = pltpu.VMEM, pltpu.SemaphoreType.DMA
    pn, rn, hn = max(parts - 1, 1), max(reps - 1, 1), max(head_n - 1, 1)
    scratch = [
        vmem((groups, parts, per, block, width), bf16),
        vmem((groups, parts, per, block, width), bf16),
        vmem((groups, parts, per, block, width), bf16),
        vmem((groups, pn, per, block, width), bf16),
        vmem((groups, parts, per, block, width), bf16),
        vmem((2, per, gate_part, width), f32),
        vmem((per, down_part, hidden), f32),
        vmem((groups + 1, 2, per, hidden, width), bf16),
        vmem((groups + 1, per, width, hidden), bf16),
        vmem((per, hidden, width), bf16),
        vmem((2, per, hidden, width), f32),
        vmem((per, hidden, width), f32),
        vmem((per, width, hidden), f32),
        vmem((groups, rn, 2, per, gate_part, width), bf16),
        vmem((groups, rn, 2, per, gate_part, width), bf16),
        vmem((groups, rn, per, down_part, hidden), bf16),
        vmem((groups, rn, per, down_part, hidden), bf16),
        vmem((groups, block, width // 2), f32),
        vmem((groups, hn, block, width // 2), f32),
        dma((groups, 3, pn)), dma((groups, 3, pn)),
        dma((3, pn)), dma((3, pn)),
        dma((groups, pn)), dma((groups, pn)),
        dma((3, pn)), dma((3, pn)),
        dma((groups, 2, rn)), dma((groups, 2, rn)),
        dma((groups + 1, 2, rn)), dma((groups + 1, 2, rn)),
        dma((groups, hn)), dma((groups, hn)),
    ]
    whole = pl.BlockSpec(memory_space=pltpu.VMEM)
    flops = groups * heads * 9 * 2 * block * width * hidden
    return pl.pallas_call(
        functools.partial(kernel, (tok_n, head_n, parts, reps, per)),
        out_shape=(
            jax.ShapeDtypeStruct(queries.shape, bf16),
            jax.ShapeDtypeStruct(w_gate.shape, f32),
            jax.ShapeDtypeStruct(w_up.shape, f32),
            jax.ShapeDtypeStruct(w_down.shape, f32),
        ),
        in_specs=[whole] * 8,
        out_specs=(whole,) * 4,
        scratch_shapes=scratch,
        cost_estimate=pl.CostEstimate(
            flops=flops, bytes_accessed=8 * queries.size, transcendentals=0
        ),
        compiler_params=pltpu.CompilerParams(
            collective_id=0, has_side_effects=True, vmem_limit_bytes=56 * 1024 * 1024
        ),
    )(key_vectors, errors, queries, mask[..., None], out_gain, w_gate, w_up, w_down)


def solution(mesh):
    tokens = P(None, "head", "tok", None)
    weight = P("head", "tok", None)
    in_specs = (
        tokens, tokens, tokens, P(None, "head", "tok"), P(), P("head", None),
        weight, weight, weight,
    )
    return jax.shard_map(
        on_device, mesh=mesh, in_specs=in_specs,
        out_specs=(tokens, weight, weight, weight), check_vma=False,
    )
```

```python
import functools

import jax
import jax.numpy as jnp
from jax import lax
from jax.experimental import pallas as pl
from jax.experimental.pallas import tpu as pltpu
from jax.sharding import PartitionSpec as P

epsilon = 1e-06
MESH = pl.DeviceIdType.MESH
NT = (((1,), (1,)), ((), ()))


def dot_nt(left, right):
    return lax.dot_general(left, right, NT, preferred_element_type=jnp.float32)


def dot_nn(left, right):
    return jnp.dot(left, right, preferred_element_type=jnp.float32)


def sigmoid(x):
    return 0.5 * jnp.tanh(0.5 * x) + 0.5


def renorm(previous, stepped):
    kept = jnp.sqrt(jnp.mean(previous * previous, axis=-1, keepdims=True))
    return (
        stepped
        * kept
        * lax.rsqrt(jnp.mean(stepped * stepped, axis=-1, keepdims=True) + epsilon)
    )


def flip(index, step, count):
    result = index
    bit = 1
    while bit < count:
        on = lax.rem(lax.div(index, bit), 2)
        chosen = (step // bit) % 2 if isinstance(step, int) else lax.rem(lax.div(step, bit), 2)
        result = result + bit * chosen * (1 - 2 * on)
        bit *= 2
    return result


def kernel(
    dims,
    k_ref, e_ref, q_ref, mask_ref, wg_ref, wu_ref, wd_ref,
    out_ref, scale_ref, fg_ref, fu_ref, fd_ref,
    kbuf, ebuf, qbuf, o_send, wg_c, wu_c, wd_c, fin_g, fin_u, fin_d,
    gu_m, d_m, gu_b, d_b, dt_b,
    dgu, ddt, dd,
    rs_send, rs_recv, rsd_send, rsd_recv,
    ms_send, ms_recv,
    tok_s, tok_r, w_s, w_r, o_s, o_r, f_s, f_r,
    rs_s, rs_r, ag_s, ag_r, ms_s, ms_r,
):
    tok_n, head_n, parts, reps, per = dims
    groups = k_ref.shape[0]
    heads = k_ref.shape[1]
    width = k_ref.shape[3]
    hidden = wd_ref.shape[2]
    gate_rows, down_rows = wg_ref.shape[1], wd_ref.shape[1]
    gate_part, down_part = parts * gate_rows, parts * down_rows
    tok = lax.axis_index("tok")
    hid = lax.axis_index("head")
    mine = lax.rem(tok, parts)
    rep = tok // parts

    part_peers = [flip(mine, s, parts) for s in range(1, parts)]
    rep_peers = [flip(rep, s, reps) for s in range(1, reps)]
    head_peers = [flip(hid, s, head_n) for s in range(1, head_n)]

    def part_dev(index):
        return (hid, rep * parts + index)

    def rep_dev(index):
        return (hid, index * parts + mine)

    barrier = pltpu.get_barrier_semaphore()
    everyone = (
        [part_dev(j) for j in part_peers]
        + [rep_dev(j) for j in rep_peers]
        + [(j, tok) for j in head_peers]
    )
    for device in everyone:
        pl.semaphore_signal(barrier, inc=1, device_id=device, device_id_type=MESH)
    wg_c[...] = wg_ref[...].astype(wg_c.dtype)
    wu_c[...] = wu_ref[...].astype(wu_c.dtype)
    wd_c[...] = wd_ref[...].astype(wd_c.dtype)
    pl.semaphore_wait(barrier, len(everyone))

    pending = []

    def remote(src, dst, send, recv, device):
        return pltpu.make_async_remote_copy(
            src_ref=src, dst_ref=dst, send_sem=send, recv_sem=recv,
            device_id=device, device_id_type=MESH,
        )

    def push(src, dst, send, recv, device):
        copy = remote(src, dst, send, recv, device)
        copy.start()
        pending.append(copy)

    def rows_of(index, size):
        return pl.ds(pl.multiple_of(index * size, size), size)

    def heads_of(index):
        return pl.ds(index * per, per)

    tokens = ((k_ref, kbuf), (e_ref, ebuf), (q_ref, qbuf))

    def send_tokens(group, kinds):
        for s, j in enumerate(part_peers):
            for kind in kinds:
                src, dst = tokens[kind]
                push(
                    src.at[group, heads_of(j)], dst.at[group, mine],
                    tok_s.at[group, kind, s], tok_r.at[group, kind, s], part_dev(j),
                )

    def wait_tokens(group, kinds, source, s):
        for kind in kinds:
            dst = tokens[kind][1].at[group, source]
            remote(
                dst, dst, tok_s.at[group, kind, s], tok_r.at[group, kind, s], part_dev(source)
            ).wait_recv()

    narrow_gate = wg_c.dtype == jnp.bfloat16
    narrow_down = wd_c.dtype == jnp.bfloat16

    def owned(stage, index):
        row = rep * parts + index
        if narrow_gate:
            gate = [gu_b.at[stage, i, :, rows_of(row, gate_rows)] for i in range(2)]
        else:
            gate = [gu_m.at[i, :, rows_of(index, gate_rows)] for i in range(2)]
        if narrow_down:
            return gate + [d_b.at[stage, :, rows_of(row, down_rows)]]
        return gate + [d_m.at[:, rows_of(index, down_rows)]]

    for s, j in enumerate(part_peers):
        for kind, (src, dst) in enumerate(zip((wg_c, wu_c, wd_c), owned(0, mine))):
            push(src.at[heads_of(j)], dst, w_s.at[kind, s], w_r.at[kind, s], part_dev(j))
    send_tokens(0, (0, 1))
    for src, dst in zip((wg_c, wu_c, wd_c), owned(0, mine)):
        dst[...] = src[heads_of(mine)]
    for group in range(groups):
        for src, dst in tokens:
            dst[group, mine] = src[group, heads_of(mine)]

    def share(stage):
        gate_own, down_own = rows_of(rep, gate_part), rows_of(rep, down_part)
        if stage > 0 or not narrow_gate:
            gu_b[stage, :, :, gate_own] = gu_m[...].astype(jnp.bfloat16)
        if stage > 0 or not narrow_down:
            d_b[stage, :, down_own] = d_m[...].astype(jnp.bfloat16)
        for s, j in enumerate(rep_peers):
            gu = gu_b.at[stage, :, :, gate_own]
            push(gu, gu, ag_s.at[stage, 0, s], ag_r.at[stage, 0, s], rep_dev(j))
            down = d_b.at[stage, :, down_own]
            push(down, down, ag_s.at[stage, 1, s], ag_r.at[stage, 1, s], rep_dev(j))

    def wait_share(stage):
        for s in range(reps - 1):
            j = rep_peers[s]
            gu = gu_b.at[stage, :, :, rows_of(j, gate_part)]
            remote(gu, gu, ag_s.at[stage, 0, s], ag_r.at[stage, 0, s], rep_dev(j)).wait_recv()
            down = d_b.at[stage, :, rows_of(j, down_part)]
            remote(down, down, ag_s.at[stage, 1, s], ag_r.at[stage, 1, s], rep_dev(j)).wait_recv()

    def update(group):
        dgu[...] = jnp.zeros_like(dgu)
        ddt[...] = jnp.zeros_like(ddt)
        for h in range(per):
            dt_b[h] = d_b[group, h].astype(jnp.float32).T.astype(jnp.bfloat16)

        def one(source):
            for h in range(per):
                key = kbuf[group, source, h]
                err = ebuf[group, source, h]
                a = dot_nt(gu_b[group, 0, h], key)
                b = dot_nt(gu_b[group, 1, h], key)
                r = dot_nt(dt_b[h], err)
                sg = sigmoid(a)
                act = a * sg
                ddt[h] += dot_nn((act * b).astype(jnp.bfloat16), err)
                da = (r * b * sg * (1.0 + a * (1.0 - sg))).astype(jnp.bfloat16)
                dgu[0, h] += dot_nn(da, key)
                dgu[1, h] += dot_nn((r * act).astype(jnp.bfloat16), key)

        def step(s, carry):
            source = flip(mine, s, parts)

            @pl.when(s > 0)
            def _():
                wait_tokens(group, (0, 1), source, s - 1)

            one(source)
            return carry

        lax.fori_loop(0, parts, step, 0)
        for h in range(per):
            dd[h] = ddt[h].T

    def scatter(group):
        for s, j in enumerate(rep_peers):
            rs_send[group, s] = dgu[:, :, rows_of(j, gate_part)].astype(jnp.bfloat16)
            push(
                rs_send.at[group, s], rs_recv.at[group, s],
                rs_s.at[group, 0, s], rs_r.at[group, 0, s], rep_dev(j),
            )
            rsd_send[group, s] = dd[:, rows_of(j, down_part)].astype(jnp.bfloat16)
            push(
                rsd_send.at[group, s], rsd_recv.at[group, s],
                rs_s.at[group, 1, s], rs_r.at[group, 1, s], rep_dev(j),
            )

    def settle(group):
        gate = gu_m[...] + dgu[:, :, rows_of(rep, gate_part)]
        down = d_m[...] + dd[:, rows_of(rep, down_part)]
        for s in range(reps - 1):
            j = rep_peers[s]
            got = rs_recv.at[group, s]
            remote(got, got, rs_s.at[group, 0, s], rs_r.at[group, 0, s], rep_dev(j)).wait_recv()
            gate = gate + got[...].astype(jnp.float32)
            got = rsd_recv.at[group, s]
            remote(got, got, rs_s.at[group, 1, s], rs_r.at[group, 1, s], rep_dev(j)).wait_recv()
            down = down + got[...].astype(jnp.float32)
        gu_m[...] = renorm(gu_m[...], gate)
        d_m[...] = renorm(d_m[...], down)

    def apply(group):
        stage = group + 1

        def one(source, into):
            for h in range(per):
                query = qbuf[group, source, h]
                a = dot_nt(query, gu_b[stage, 0, h])
                b = dot_nt(query, gu_b[stage, 1, h])
                hid_act = (a * sigmoid(a) * b).astype(jnp.bfloat16)
                into[h] = dot_nt(hid_act, d_b[stage, h]).astype(jnp.bfloat16)

        def out_copy(s):
            return remote(
                o_send.at[group, s], out_ref.at[group, heads_of(mine)],
                o_s.at[group, s], o_r.at[group, s], part_dev(flip(mine, s + 1, parts)),
            )

        def step(i, carry):
            s = parts - 2 - i
            source = flip(mine, s + 1, parts)
            wait_tokens(group, (2,), source, s)
            one(source, o_send.at[group, s])
            out_copy(s).start()
            return carry

        lax.fori_loop(0, parts - 1, step, 0)
        one(mine, out_ref.at[group, heads_of(mine)])
        for s in range(parts - 1):
            pending.append(out_copy(s))

    def finish(group):
        for s, j in enumerate(part_peers):
            got = out_ref.at[group, heads_of(j)]
            remote(got, got, o_s.at[group, s], o_r.at[group, s], part_dev(j)).wait_recv()
        half = width // 2
        total = jnp.zeros((k_ref.shape[2], half), jnp.float32)
        for head in range(heads):
            o = out_ref[group, head].astype(jnp.float32)
            total = total + (o[:, :half] * o[:, :half] + o[:, half:] * o[:, half:])
        ms_send[group] = total
        for s, j in enumerate(head_peers):
            push(
                ms_send.at[group], ms_recv.at[group, s],
                ms_s.at[group, s], ms_r.at[group, s], (j, tok),
            )
        for s in range(head_n - 1):
            j = head_peers[s]
            got = ms_recv.at[group, s]
            remote(got, got, ms_s.at[group, s], ms_r.at[group, s], (j, tok)).wait_recv()
            total = total + got[...]
        mean = jnp.sum(total, axis=1, keepdims=True) / (head_n * heads * width)
        scale = lax.rsqrt(mean + epsilon) * mask_ref[group]
        scale_ref[group] = jnp.broadcast_to(scale, scale_ref.shape[1:])

    for s, j in enumerate(part_peers):
        for kind, got in enumerate(owned(0, j)):
            remote(got, got, w_s.at[kind, s], w_r.at[kind, s], part_dev(j)).wait_recv()
    share(0)
    if narrow_gate:
        gu_m[...] = gu_b[0, :, :, rows_of(rep, gate_part)].astype(jnp.float32)
    if narrow_down:
        d_m[...] = d_b[0, :, rows_of(rep, down_part)].astype(jnp.float32)
    wait_share(0)
    finals = (fin_g, fin_u, fin_d)
    for group in range(groups):
        update(group)
        scatter(group)
        if group + 1 < groups:
            send_tokens(group + 1, (0, 1))
        if group > 0:
            send_tokens(group, (2,))
            apply(group - 1)
        settle(group)
        share(group + 1)
        if group == 0:
            send_tokens(0, (2,))
        if group > 0:
            finish(group - 1)
        wait_share(group + 1)
    apply(groups - 1)
    for s, j in enumerate(part_peers):
        for kind, (src, dst) in enumerate(zip(owned(groups, j), finals)):
            push(src, dst.at[heads_of(mine)], f_s.at[kind, s], f_r.at[kind, s], part_dev(j))
    for src, dst in zip(owned(groups, mine), finals):
        dst[heads_of(mine)] = src[...]
    finish(groups - 1)
    for s, j in enumerate(part_peers):
        for kind, dst in enumerate(finals):
            got = dst.at[heads_of(j)]
            remote(got, got, f_s.at[kind, s], f_r.at[kind, s], part_dev(j)).wait_recv()
    fg_ref[...] = fin_g[...].astype(jnp.float32)
    fu_ref[...] = fin_u[...].astype(jnp.float32)
    fd_ref[...] = fin_d[...].astype(jnp.float32)
    for copy in pending:
        copy.wait_send()


def on_device(
    queries, key_vectors, value_vectors, step_rates, counts, out_gain, w_gate, w_up, w_down
):
    tok_n, head_n = lax.axis_size("tok"), lax.axis_size("head")
    groups, heads, block, width = key_vectors.shape
    hidden = w_down.shape[2]
    parts = min(heads, tok_n)
    per, reps = heads // parts, tok_n // parts
    gate_rows, down_rows = w_gate.shape[1], w_down.shape[1]
    gate_part, down_part = parts * gate_rows, parts * down_rows
    grad_scale = float(tok_n * block) ** (-0.5)
    own = lax.dynamic_slice_in_dim(counts, lax.axis_index("tok"), 1, 1)
    mask = (jnp.arange(block, dtype=jnp.int32)[None, :] < own).astype(jnp.float32)
    rate = step_rates.astype(jnp.float32) * grad_scale * mask[:, None, :]
    errors = (value_vectors.astype(jnp.float32) * rate[..., None]).astype(jnp.bfloat16)

    bf16, f32 = jnp.bfloat16, jnp.float32

    def wire(rows):
        return bf16 if rows % 16 == 0 else f32

    vmem, dma = pltpu.VMEM, pltpu.SemaphoreType.DMA
    pn, rn, hn = max(parts - 1, 1), max(reps - 1, 1), max(head_n - 1, 1)
    scratch = [
        vmem((groups, parts, per, block, width), bf16),
        vmem((groups, parts, per, block, width), bf16),
        vmem((groups, parts, per, block, width), bf16),
        vmem((groups, pn, per, block, width), bf16),
        vmem(w_gate.shape, wire(gate_rows)),
        vmem(w_up.shape, wire(gate_rows)),
        vmem(w_down.shape, wire(down_rows)),
        vmem(w_gate.shape, wire(gate_rows)),
        vmem(w_up.shape, wire(gate_rows)),
        vmem(w_down.shape, wire(down_rows)),
        vmem((2, per, gate_part, width), f32),
        vmem((per, down_part, hidden), f32),
        vmem((groups + 1, 2, per, hidden, width), bf16),
        vmem((groups + 1, per, width, hidden), bf16),
        vmem((per, hidden, width), bf16),
        vmem((2, per, hidden, width), f32),
        vmem((per, hidden, width), f32),
        vmem((per, width, hidden), f32),
        vmem((groups, rn, 2, per, gate_part, width), bf16),
        vmem((groups, rn, 2, per, gate_part, width), bf16),
        vmem((groups, rn, per, down_part, hidden), bf16),
        vmem((groups, rn, per, down_part, hidden), bf16),
        vmem((groups, block, width // 2), f32),
        vmem((groups, hn, block, width // 2), f32),
        dma((groups, 3, pn)), dma((groups, 3, pn)),
        dma((3, pn)), dma((3, pn)),
        dma((groups, pn)), dma((groups, pn)),
        dma((3, pn)), dma((3, pn)),
        dma((groups, 2, rn)), dma((groups, 2, rn)),
        dma((groups + 1, 2, rn)), dma((groups + 1, 2, rn)),
        dma((groups, hn)), dma((groups, hn)),
    ]
    whole = pl.BlockSpec(memory_space=pltpu.VMEM)
    flops = groups * heads * 9 * 2 * block * width * hidden
    produced, scale, final_gate, final_up, final_down = pl.pallas_call(
        functools.partial(kernel, (tok_n, head_n, parts, reps, per)),
        out_shape=(
            jax.ShapeDtypeStruct(queries.shape, bf16),
            jax.ShapeDtypeStruct((groups, block, 128), f32),
            jax.ShapeDtypeStruct(w_gate.shape, f32),
            jax.ShapeDtypeStruct(w_up.shape, f32),
            jax.ShapeDtypeStruct(w_down.shape, f32),
        ),
        in_specs=[whole] * 7,
        out_specs=(whole,) * 5,
        scratch_shapes=scratch,
        cost_estimate=pl.CostEstimate(
            flops=flops, bytes_accessed=8 * queries.size, transcendentals=0
        ),
        compiler_params=pltpu.CompilerParams(
            collective_id=0, has_side_effects=True, vmem_limit_bytes=56 * 1024 * 1024
        ),
    )(key_vectors, errors, queries, mask[..., None], w_gate, w_up, w_down)
    mixed = (
        produced.astype(f32) * out_gain[None, :, None, :] * scale[:, None, :, :1]
    ).astype(bf16)
    return mixed, final_gate, final_up, final_down


def solution(mesh):
    tokens = P(None, "head", "tok", None)
    weight = P("head", "tok", None)
    in_specs = (
        tokens, tokens, tokens, P(None, "head", "tok"), P(), P("head", None),
        weight, weight, weight,
    )
    return jax.shard_map(
        on_device, mesh=mesh, in_specs=in_specs,
        out_specs=(tokens, weight, weight, weight), check_vma=False,
    )
```

```python
import functools

import jax
import jax.numpy as jnp
from jax import lax
from jax.experimental import pallas as pl
from jax.experimental.pallas import tpu as pltpu
from jax.sharding import PartitionSpec as P

epsilon = 1e-06
MESH = pl.DeviceIdType.MESH
NT = (((1,), (1,)), ((), ()))


def dot_nt(left, right):
    return lax.dot_general(left, right, NT, preferred_element_type=jnp.float32)


def dot_nn(left, right):
    return jnp.dot(left, right, preferred_element_type=jnp.float32)


def sigmoid(x):
    return 0.5 * jnp.tanh(0.5 * x) + 0.5


def renorm(previous, stepped):
    kept = jnp.sqrt(jnp.mean(previous * previous, axis=-1, keepdims=True))
    return (
        stepped
        * kept
        * lax.rsqrt(jnp.mean(stepped * stepped, axis=-1, keepdims=True) + epsilon)
    )


def flip(index, step, count):
    result = index
    bit = 1
    while bit < count:
        on = lax.rem(lax.div(index, bit), 2)
        chosen = (step // bit) % 2 if isinstance(step, int) else lax.rem(lax.div(step, bit), 2)
        result = result + bit * chosen * (1 - 2 * on)
        bit *= 2
    return result


def kernel(
    dims,
    cnt_ref, k_ref, v_ref, q_ref, rate_ref, wg_ref, wu_ref, wd_ref,
    out_ref, scale_ref, fg_ref, fu_ref, fd_ref,
    e_src, rate_s, kbuf, ebuf, qbuf, o_send, wg_c, wu_c, wd_c, fin_g, fin_u, fin_d,
    gu_m, d_m, gu_b, d_b, dt_b,
    dgu, ddt, dd,
    rs_send, rs_recv, rsd_send, rsd_recv,
    ms_send, ms_recv,
    own_s, tok_s, tok_r, w_s, w_r, o_s, o_r, f_s, f_r,
    rs_s, rs_r, ag_s, ag_r, ms_s, ms_r,
):
    tok_n, head_n, parts, reps, per, grad_scale = dims
    block = k_ref.shape[2]
    groups = k_ref.shape[0]
    heads = k_ref.shape[1]
    width = k_ref.shape[3]
    hidden = wd_ref.shape[2]
    gate_rows, down_rows = wg_ref.shape[1], wd_ref.shape[1]
    gate_part, down_part = parts * gate_rows, parts * down_rows
    tok = lax.axis_index("tok")
    hid = lax.axis_index("head")
    mine = lax.rem(tok, parts)
    rep = tok // parts

    part_peers = [flip(mine, s, parts) for s in range(1, parts)]
    rep_peers = [flip(rep, s, reps) for s in range(1, reps)]
    head_peers = [flip(hid, s, head_n) for s in range(1, head_n)]

    def part_dev(index):
        return (hid, rep * parts + index)

    def rep_dev(index):
        return (hid, index * parts + mine)

    barrier = pltpu.get_barrier_semaphore()
    everyone = (
        [part_dev(j) for j in part_peers]
        + [rep_dev(j) for j in rep_peers]
        + [(j, tok) for j in head_peers]
    )
    for device in everyone:
        pl.semaphore_signal(barrier, inc=1, device_id=device, device_id_type=MESH)
    wg_c[...] = wg_ref[...].astype(wg_c.dtype)
    wu_c[...] = wu_ref[...].astype(wu_c.dtype)
    wd_c[...] = wd_ref[...].astype(wd_c.dtype)

    def weigh(group):
        count = cnt_ref[group, tok]
        valid = (lax.broadcasted_iota(jnp.int32, (1, block), 1) < count).astype(jnp.float32)
        rate_s[...] = jnp.zeros_like(rate_s)
        rate_s[:heads] = rate_ref[group].astype(jnp.float32) * grad_scale * valid
        columns = rate_s[...].T
        for head in range(heads):
            value = v_ref[group, head].astype(jnp.float32)
            e_src[group, head] = (value * columns[:, head : head + 1]).astype(jnp.bfloat16)

    weigh(0)
    pl.semaphore_wait(barrier, len(everyone))

    pending = []

    def remote(src, dst, send, recv, device):
        return pltpu.make_async_remote_copy(
            src_ref=src, dst_ref=dst, send_sem=send, recv_sem=recv,
            device_id=device, device_id_type=MESH,
        )

    def push(src, dst, send, recv, device):
        copy = remote(src, dst, send, recv, device)
        copy.start()
        pending.append(copy)

    def rows_of(index, size):
        return pl.ds(pl.multiple_of(index * size, size), size)

    def heads_of(index):
        return pl.ds(index * per, per)

    tokens = ((k_ref, kbuf), (e_src, ebuf), (q_ref, qbuf))

    def send_tokens(group, kinds):
        for s, j in enumerate(part_peers):
            for kind in kinds:
                src, dst = tokens[kind]
                push(
                    src.at[group, heads_of(j)], dst.at[group, mine],
                    tok_s.at[group, kind, s], tok_r.at[group, kind, s], part_dev(j),
                )

    def wait_tokens(group, kinds, source, s):
        for kind in kinds:
            dst = tokens[kind][1].at[group, source]
            remote(
                dst, dst, tok_s.at[group, kind, s], tok_r.at[group, kind, s], part_dev(source)
            ).wait_recv()

    narrow_gate = wg_c.dtype == jnp.bfloat16
    narrow_down = wd_c.dtype == jnp.bfloat16

    def owned(stage, index):
        row = rep * parts + index
        if narrow_gate:
            gate = [gu_b.at[stage, i, :, rows_of(row, gate_rows)] for i in range(2)]
        else:
            gate = [gu_m.at[i, :, rows_of(index, gate_rows)] for i in range(2)]
        if narrow_down:
            return gate + [d_b.at[stage, :, rows_of(row, down_rows)]]
        return gate + [d_m.at[:, rows_of(index, down_rows)]]

    for s, j in enumerate(part_peers):
        for kind, (src, dst) in enumerate(zip((wg_c, wu_c, wd_c), owned(0, mine))):
            push(src.at[heads_of(j)], dst, w_s.at[kind, s], w_r.at[kind, s], part_dev(j))
    send_tokens(0, (0, 1))
    for src, dst in zip((wg_c, wu_c, wd_c), owned(0, mine)):
        dst[...] = src[heads_of(mine)]
    own_copies = []
    for group in range(groups):
        for kind in (0, 2):
            src, dst = tokens[kind]
            copy = pltpu.make_async_copy(
                src.at[group, heads_of(mine)], dst.at[group, mine], own_s.at[group, kind]
            )
            copy.start()
            own_copies.append(copy)
    ebuf[0, mine] = e_src[0, heads_of(mine)]
    for group in range(1, groups):
        weigh(group)
        ebuf[group, mine] = e_src[group, heads_of(mine)]
    for copy in own_copies:
        copy.wait()

    def share_gate(stage):
        own = rows_of(rep, gate_part)
        if stage > 0 or not narrow_gate:
            gu_b[stage, :, :, own] = gu_m[...].astype(jnp.bfloat16)
        for s, j in enumerate(rep_peers):
            gu = gu_b.at[stage, :, :, own]
            push(gu, gu, ag_s.at[stage, 0, s], ag_r.at[stage, 0, s], rep_dev(j))

    def share_down(stage):
        own = rows_of(rep, down_part)
        if stage > 0 or not narrow_down:
            d_b[stage, :, own] = d_m[...].astype(jnp.bfloat16)
        for s, j in enumerate(rep_peers):
            down = d_b.at[stage, :, own]
            push(down, down, ag_s.at[stage, 1, s], ag_r.at[stage, 1, s], rep_dev(j))

    def wait_share(stage):
        for s in range(reps - 1):
            j = rep_peers[s]
            gu = gu_b.at[stage, :, :, rows_of(j, gate_part)]
            remote(gu, gu, ag_s.at[stage, 0, s], ag_r.at[stage, 0, s], rep_dev(j)).wait_recv()
            down = d_b.at[stage, :, rows_of(j, down_part)]
            remote(down, down, ag_s.at[stage, 1, s], ag_r.at[stage, 1, s], rep_dev(j)).wait_recv()

    def update(group):
        dgu[...] = jnp.zeros_like(dgu)
        ddt[...] = jnp.zeros_like(ddt)
        for h in range(per):
            dt_b[h] = d_b[group, h].astype(jnp.float32).T.astype(jnp.bfloat16)

        def one(source, rows):
            for h in range(per):
                key = kbuf[group, source, h]
                err = ebuf[group, source, h]
                a = dot_nt(gu_b[group, 0, h, rows], key)
                b = dot_nt(gu_b[group, 1, h, rows], key)
                r = dot_nt(dt_b[h, rows], err)
                sg = sigmoid(a)
                act = a * sg
                ddt[h, rows] += dot_nn((act * b).astype(jnp.bfloat16), err)
                da = (r * b * sg * (1.0 + a * (1.0 - sg))).astype(jnp.bfloat16)
                dgu[0, h, rows] += dot_nn(da, key)
                dgu[1, h, rows] += dot_nn((r * act).astype(jnp.bfloat16), key)

        def one_pass(rows, first):
            def step(s, carry):
                source = flip(mine, s, parts)
                if first:

                    @pl.when(s > 0)
                    def _():
                        wait_tokens(group, (0, 1), source, s - 1)

                one(source, rows)
                return carry

            lax.fori_loop(0, parts, step, 0)

        for s, j in enumerate(rep_peers):
            rows = rows_of(j, gate_part)
            one_pass(rows, s == 0)
            rs_send[group, s] = dgu[:, :, rows].astype(jnp.bfloat16)
            push(
                rs_send.at[group, s], rs_recv.at[group, s],
                rs_s.at[group, 0, s], rs_r.at[group, 0, s], rep_dev(j),
            )
        one_pass(rows_of(rep, gate_part), not rep_peers)
        for h in range(per):
            dd[h] = ddt[h].T
        for s, j in enumerate(rep_peers):
            rsd_send[group, s] = dd[:, rows_of(j, down_part)].astype(jnp.bfloat16)
            push(
                rsd_send.at[group, s], rsd_recv.at[group, s],
                rs_s.at[group, 1, s], rs_r.at[group, 1, s], rep_dev(j),
            )

    def settle_gate(group):
        gate = gu_m[...] + dgu[:, :, rows_of(rep, gate_part)]
        for s, j in enumerate(rep_peers):
            got = rs_recv.at[group, s]
            remote(got, got, rs_s.at[group, 0, s], rs_r.at[group, 0, s], rep_dev(j)).wait_recv()
            gate = gate + got[...].astype(jnp.float32)
        gu_m[...] = renorm(gu_m[...], gate)

    def settle_down(group):
        down = d_m[...] + dd[:, rows_of(rep, down_part)]
        for s, j in enumerate(rep_peers):
            got = rsd_recv.at[group, s]
            remote(got, got, rs_s.at[group, 1, s], rs_r.at[group, 1, s], rep_dev(j)).wait_recv()
            down = down + got[...].astype(jnp.float32)
        d_m[...] = renorm(d_m[...], down)

    def apply(group):
        stage = group + 1

        def one(source, into):
            for h in range(per):
                query = qbuf[group, source, h]
                a = dot_nt(query, gu_b[stage, 0, h])
                b = dot_nt(query, gu_b[stage, 1, h])
                hid_act = (a * sigmoid(a) * b).astype(jnp.bfloat16)
                into[h] = dot_nt(hid_act, d_b[stage, h]).astype(jnp.bfloat16)

        def out_copy(s):
            return remote(
                o_send.at[group, s], out_ref.at[group, heads_of(mine)],
                o_s.at[group, s], o_r.at[group, s], part_dev(flip(mine, s + 1, parts)),
            )

        def step(i, carry):
            s = parts - 2 - i
            source = flip(mine, s + 1, parts)
            wait_tokens(group, (2,), source, s)
            one(source, o_send.at[group, s])
            out_copy(s).start()
            return carry

        lax.fori_loop(0, parts - 1, step, 0)
        one(mine, out_ref.at[group, heads_of(mine)])
        for s in range(parts - 1):
            pending.append(out_copy(s))

    def finish(group):
        for s, j in enumerate(part_peers):
            got = out_ref.at[group, heads_of(j)]
            remote(got, got, o_s.at[group, s], o_r.at[group, s], part_dev(j)).wait_recv()
        half = width // 2
        total = jnp.zeros((k_ref.shape[2], half), jnp.float32)
        for head in range(heads):
            o = out_ref[group, head].astype(jnp.float32)
            total = total + (o[:, :half] * o[:, :half] + o[:, half:] * o[:, half:])
        ms_send[group] = total
        for s, j in enumerate(head_peers):
            push(
                ms_send.at[group], ms_recv.at[group, s],
                ms_s.at[group, s], ms_r.at[group, s], (j, tok),
            )
        for s in range(head_n - 1):
            j = head_peers[s]
            got = ms_recv.at[group, s]
            remote(got, got, ms_s.at[group, s], ms_r.at[group, s], (j, tok)).wait_recv()
            total = total + got[...]
        mean = jnp.sum(total, axis=1, keepdims=True) / (head_n * heads * width)
        scale = lax.rsqrt(mean + epsilon) * (
            lax.broadcasted_iota(jnp.int32, (block, 1), 0) < cnt_ref[group, tok]
        ).astype(jnp.float32)
        scale_ref[group] = scale

    for s, j in enumerate(part_peers):
        for kind, got in enumerate(owned(0, j)):
            remote(got, got, w_s.at[kind, s], w_r.at[kind, s], part_dev(j)).wait_recv()
    share_gate(0)
    share_down(0)
    if narrow_gate:
        gu_m[...] = gu_b[0, :, :, rows_of(rep, gate_part)].astype(jnp.float32)
    if narrow_down:
        d_m[...] = d_b[0, :, rows_of(rep, down_part)].astype(jnp.float32)
    wait_share(0)
    finals = (fin_g, fin_u, fin_d)
    for group in range(groups):
        update(group)
        if group + 1 < groups:
            send_tokens(group + 1, (0, 1))
        if group > 0:
            send_tokens(group, (2,))
            apply(group - 1)
        settle_gate(group)
        share_gate(group + 1)
        settle_down(group)
        share_down(group + 1)
        if group == 0:
            send_tokens(0, (2,))
        if group + 1 == groups:
            for s, j in enumerate(part_peers):
                for kind, (src, dst) in enumerate(zip(owned(groups, j), finals)):
                    push(src, dst.at[heads_of(mine)], f_s.at[kind, s], f_r.at[kind, s], part_dev(j))
            for src, dst in zip(owned(groups, mine), finals):
                dst[heads_of(mine)] = src[...]
        if group > 0:
            finish(group - 1)
        wait_share(group + 1)
    apply(groups - 1)
    finish(groups - 1)
    for s, j in enumerate(part_peers):
        for kind, dst in enumerate(finals):
            got = dst.at[heads_of(j)]
            remote(got, got, f_s.at[kind, s], f_r.at[kind, s], part_dev(j)).wait_recv()
    fg_ref[...] = fin_g[...].astype(jnp.float32)
    fu_ref[...] = fin_u[...].astype(jnp.float32)
    fd_ref[...] = fin_d[...].astype(jnp.float32)
    for copy in pending:
        copy.wait_send()


def on_device(
    queries, key_vectors, value_vectors, step_rates, counts, out_gain, w_gate, w_up, w_down
):
    tok_n, head_n = lax.axis_size("tok"), lax.axis_size("head")
    groups, heads, block, width = key_vectors.shape
    hidden = w_down.shape[2]
    parts = min(heads, tok_n)
    per, reps = heads // parts, tok_n // parts
    gate_rows, down_rows = w_gate.shape[1], w_down.shape[1]
    gate_part, down_part = parts * gate_rows, parts * down_rows
    grad_scale = float(tok_n * block) ** (-0.5)
    bf16, f32 = jnp.bfloat16, jnp.float32

    def wire(rows):
        return bf16 if rows % 16 == 0 else f32

    vmem, dma = pltpu.VMEM, pltpu.SemaphoreType.DMA
    pn, rn, hn = max(parts - 1, 1), max(reps - 1, 1), max(head_n - 1, 1)
    scratch = [
        vmem(value_vectors.shape, bf16),
        vmem((max(8, heads), block), f32),
        vmem((groups, parts, per, block, width), bf16),
        vmem((groups, parts, per, block, width), bf16),
        vmem((groups, parts, per, block, width), bf16),
        vmem((groups, pn, per, block, width), bf16),
        vmem(w_gate.shape, wire(gate_rows)),
        vmem(w_up.shape, wire(gate_rows)),
        vmem(w_down.shape, wire(down_rows)),
        vmem(w_gate.shape, wire(gate_rows)),
        vmem(w_up.shape, wire(gate_rows)),
        vmem(w_down.shape, wire(down_rows)),
        vmem((2, per, gate_part, width), f32),
        vmem((per, down_part, hidden), f32),
        vmem((groups + 1, 2, per, hidden, width), bf16),
        vmem((groups + 1, per, width, hidden), bf16),
        vmem((per, hidden, width), bf16),
        vmem((2, per, hidden, width), f32),
        vmem((per, hidden, width), f32),
        vmem((per, width, hidden), f32),
        vmem((groups, rn, 2, per, gate_part, width), bf16),
        vmem((groups, rn, 2, per, gate_part, width), bf16),
        vmem((groups, rn, per, down_part, hidden), bf16),
        vmem((groups, rn, per, down_part, hidden), bf16),
        vmem((groups, block, width // 2), f32),
        vmem((groups, hn, block, width // 2), f32),
        dma((groups, 3)),
        dma((groups, 3, pn)), dma((groups, 3, pn)),
        dma((3, pn)), dma((3, pn)),
        dma((groups, pn)), dma((groups, pn)),
        dma((3, pn)), dma((3, pn)),
        dma((groups, 2, rn)), dma((groups, 2, rn)),
        dma((groups + 1, 2, rn)), dma((groups + 1, 2, rn)),
        dma((groups, hn)), dma((groups, hn)),
    ]
    whole = pl.BlockSpec(memory_space=pltpu.VMEM)
    hbm = pl.BlockSpec(memory_space=pl.ANY)
    flops = groups * heads * 9 * 2 * block * width * hidden
    produced, scale, final_gate, final_up, final_down = pl.pallas_call(
        functools.partial(kernel, (tok_n, head_n, parts, reps, per, grad_scale)),
        out_shape=(
            jax.ShapeDtypeStruct(queries.shape, bf16),
            jax.ShapeDtypeStruct((groups, block, 1), f32),
            jax.ShapeDtypeStruct(w_gate.shape, f32),
            jax.ShapeDtypeStruct(w_up.shape, f32),
            jax.ShapeDtypeStruct(w_down.shape, f32),
        ),
        in_specs=[pl.BlockSpec(memory_space=pltpu.SMEM), hbm, whole, hbm] + [whole] * 4,
        out_specs=(whole,) * 5,
        scratch_shapes=scratch,
        cost_estimate=pl.CostEstimate(
            flops=flops, bytes_accessed=8 * queries.size, transcendentals=0
        ),
        compiler_params=pltpu.CompilerParams(
            collective_id=0, has_side_effects=True, vmem_limit_bytes=56 * 1024 * 1024
        ),
    )(counts, key_vectors, value_vectors, queries, step_rates, w_gate, w_up, w_down)
    mixed = (
        produced.astype(f32) * out_gain[None, :, None, :] * scale[:, None]
    ).astype(bf16)
    return mixed, final_gate, final_up, final_down


def solution(mesh):
    tokens = P(None, "head", "tok", None)
    weight = P("head", "tok", None)
    in_specs = (
        tokens, tokens, tokens, P(None, "head", "tok"), P(), P("head", None),
        weight, weight, weight,
    )
    return jax.shard_map(
        on_device, mesh=mesh, in_specs=in_specs,
        out_specs=(tokens, weight, weight, weight), check_vma=False,
    )
```

```python
import functools

import jax
import jax.numpy as jnp
from jax import lax
from jax.experimental import pallas as pl
from jax.experimental.pallas import tpu as pltpu
from jax.sharding import PartitionSpec as P

epsilon = 1e-06
MESH = pl.DeviceIdType.MESH
NT = (((1,), (1,)), ((), ()))


def dot_nt(left, right):
    return lax.dot_general(left, right, NT, preferred_element_type=jnp.float32)


def dot_nn(left, right):
    return jnp.dot(left, right, preferred_element_type=jnp.float32)


def sigmoid(x):
    return 0.5 * jnp.tanh(0.5 * x) + 0.5


def renorm(previous, stepped):
    kept = jnp.sqrt(jnp.mean(previous * previous, axis=-1, keepdims=True))
    return (
        stepped
        * kept
        * lax.rsqrt(jnp.mean(stepped * stepped, axis=-1, keepdims=True) + epsilon)
    )


def flip(index, step, count):
    result = index
    bit = 1
    while bit < count:
        on = lax.rem(lax.div(index, bit), 2)
        chosen = (step // bit) % 2 if isinstance(step, int) else lax.rem(lax.div(step, bit), 2)
        result = result + bit * chosen * (1 - 2 * on)
        bit *= 2
    return result


def kernel(
    dims,
    cnt_ref, k_ref, v_ref, q_ref, rate_ref, wg_ref, wu_ref, wd_ref,
    out_ref, scale_ref, fg_ref, fu_ref, fd_ref,
    e_src, rate_s, kbuf, ebuf, qbuf, o_send, wg_c, wu_c, wd_c, fin_g, fin_u, fin_d,
    gu_m, d_m, gu_b, d_b, dt_b,
    dgu, ddt, dd,
    rs_send, rs_recv, rsd_send, rsd_recv,
    ms_send, ms_recv,
    own_s, tok_s, tok_r, w_s, w_r, o_s, o_r, f_s, f_r,
    rs_s, rs_r, ag_s, ag_r, ms_s, ms_r,
):
    tok_n, head_n, parts, reps, per, grad_scale = dims
    block = k_ref.shape[2]
    groups = k_ref.shape[0]
    heads = k_ref.shape[1]
    width = k_ref.shape[3]
    hidden = wd_ref.shape[2]
    gate_rows, down_rows = wg_ref.shape[1], wd_ref.shape[1]
    gate_part, down_part = parts * gate_rows, parts * down_rows
    tok = lax.axis_index("tok")
    hid = lax.axis_index("head")
    mine = lax.rem(tok, parts)
    rep = tok // parts

    part_peers = [flip(mine, s, parts) for s in range(1, parts)]
    rep_peers = [flip(rep, s, reps) for s in range(1, reps)]
    head_peers = [flip(hid, s, head_n) for s in range(1, head_n)]

    def part_dev(index):
        return (hid, rep * parts + index)

    def rep_dev(index):
        return (hid, index * parts + mine)

    barrier = pltpu.get_barrier_semaphore()
    everyone = (
        [part_dev(j) for j in part_peers]
        + [rep_dev(j) for j in rep_peers]
        + [(j, tok) for j in head_peers]
    )
    for device in everyone:
        pl.semaphore_signal(barrier, inc=1, device_id=device, device_id_type=MESH)
    wg_c[...] = wg_ref[...].astype(wg_c.dtype)
    wu_c[...] = wu_ref[...].astype(wu_c.dtype)
    wd_c[...] = wd_ref[...].astype(wd_c.dtype)

    def weigh(group):
        count = cnt_ref[group, tok]
        valid = (lax.broadcasted_iota(jnp.int32, (1, block), 1) < count).astype(jnp.float32)
        rate_s[...] = jnp.zeros_like(rate_s)
        rate_s[:heads] = rate_ref[group].astype(jnp.float32) * grad_scale * valid
        columns = rate_s[...].T
        for head in range(heads):
            value = v_ref[group, head].astype(jnp.float32)
            e_src[group, head] = (value * columns[:, head : head + 1]).astype(jnp.bfloat16)

    weigh(0)
    pl.semaphore_wait(barrier, len(everyone))

    pending = []

    def remote(src, dst, send, recv, device):
        return pltpu.make_async_remote_copy(
            src_ref=src, dst_ref=dst, send_sem=send, recv_sem=recv,
            device_id=device, device_id_type=MESH,
        )

    def push(src, dst, send, recv, device):
        copy = remote(src, dst, send, recv, device)
        copy.start()
        pending.append(copy)

    def rows_of(index, size):
        return pl.ds(pl.multiple_of(index * size, size), size)

    def heads_of(index):
        return pl.ds(index * per, per)

    tokens = ((k_ref, kbuf), (e_src, ebuf), (q_ref, qbuf))

    def send_tokens(group, kinds):
        for s, j in enumerate(part_peers):
            for kind in kinds:
                src, dst = tokens[kind]
                push(
                    src.at[group, heads_of(j)], dst.at[group, mine],
                    tok_s.at[group, kind, s], tok_r.at[group, kind, s], part_dev(j),
                )

    def wait_tokens(group, kinds, source, s):
        for kind in kinds:
            dst = tokens[kind][1].at[group, source]
            remote(
                dst, dst, tok_s.at[group, kind, s], tok_r.at[group, kind, s], part_dev(source)
            ).wait_recv()

    narrow_gate = wg_c.dtype == jnp.bfloat16
    narrow_down = wd_c.dtype == jnp.bfloat16

    def owned(stage, index):
        row = rep * parts + index
        if narrow_gate:
            gate = [gu_b.at[stage, i, :, rows_of(row, gate_rows)] for i in range(2)]
        else:
            gate = [gu_m.at[i, :, rows_of(index, gate_rows)] for i in range(2)]
        if narrow_down:
            return gate + [d_b.at[stage, :, rows_of(row, down_rows)]]
        return gate + [d_m.at[:, rows_of(index, down_rows)]]

    for s, j in enumerate(part_peers):
        for kind, (src, dst) in enumerate(zip((wg_c, wu_c, wd_c), owned(0, mine))):
            push(src.at[heads_of(j)], dst, w_s.at[kind, s], w_r.at[kind, s], part_dev(j))
    send_tokens(0, (0, 1))
    for src, dst in zip((wg_c, wu_c, wd_c), owned(0, mine)):
        dst[...] = src[heads_of(mine)]
    own_copies = []
    for group in range(groups):
        for kind in (0, 2):
            src, dst = tokens[kind]
            copy = pltpu.make_async_copy(
                src.at[group, heads_of(mine)], dst.at[group, mine], own_s.at[group, kind]
            )
            copy.start()
            own_copies.append(copy)
    ebuf[0, mine] = e_src[0, heads_of(mine)]
    for group in range(1, groups):
        weigh(group)
        ebuf[group, mine] = e_src[group, heads_of(mine)]
    for copy in own_copies:
        copy.wait()

    def share_gate(stage):
        own = rows_of(rep, gate_part)
        if stage > 0 or not narrow_gate:
            gu_b[stage, :, :, own] = gu_m[...].astype(jnp.bfloat16)
        for s, j in enumerate(rep_peers):
            gu = gu_b.at[stage, :, :, own]
            push(gu, gu, ag_s.at[stage, 0, s], ag_r.at[stage, 0, s], rep_dev(j))

    def share_down(stage):
        own = rows_of(rep, down_part)
        if stage > 0 or not narrow_down:
            d_b[stage, :, own] = d_m[...].astype(jnp.bfloat16)
        for s, j in enumerate(rep_peers):
            down = d_b.at[stage, :, own]
            push(down, down, ag_s.at[stage, 1, s], ag_r.at[stage, 1, s], rep_dev(j))

    def wait_share(stage):
        for s in range(reps - 1):
            j = rep_peers[s]
            gu = gu_b.at[stage, :, :, rows_of(j, gate_part)]
            remote(gu, gu, ag_s.at[stage, 0, s], ag_r.at[stage, 0, s], rep_dev(j)).wait_recv()
            down = d_b.at[stage, :, rows_of(j, down_part)]
            remote(down, down, ag_s.at[stage, 1, s], ag_r.at[stage, 1, s], rep_dev(j)).wait_recv()

    def update(group, between):
        dgu[...] = jnp.zeros_like(dgu)
        ddt[...] = jnp.zeros_like(ddt)
        for h in range(per):
            dt_b[h] = d_b[group, h].astype(jnp.float32).T.astype(jnp.bfloat16)

        def one(source, rows):
            for h in range(per):
                key = kbuf[group, source, h]
                err = ebuf[group, source, h]
                a = dot_nt(gu_b[group, 0, h, rows], key)
                b = dot_nt(gu_b[group, 1, h, rows], key)
                r = dot_nt(dt_b[h, rows], err)
                sg = sigmoid(a)
                act = a * sg
                ddt[h, rows] += dot_nn((act * b).astype(jnp.bfloat16), err)
                da = (r * b * sg * (1.0 + a * (1.0 - sg))).astype(jnp.bfloat16)
                dgu[0, h, rows] += dot_nn(da, key)
                dgu[1, h, rows] += dot_nn((r * act).astype(jnp.bfloat16), key)

        def one_pass(rows, first):
            def step(s, carry):
                source = flip(mine, s, parts)
                if first:

                    @pl.when(s > 0)
                    def _():
                        wait_tokens(group, (0, 1), source, s - 1)

                one(source, rows)
                return carry

            lax.fori_loop(0, parts, step, 0)

        for s, j in enumerate(rep_peers):
            rows = rows_of(j, gate_part)
            one_pass(rows, s == 0)
            rs_send[group, s] = dgu[:, :, rows].astype(jnp.bfloat16)
            push(
                rs_send.at[group, s], rs_recv.at[group, s],
                rs_s.at[group, 0, s], rs_r.at[group, 0, s], rep_dev(j),
            )
        between()
        one_pass(rows_of(rep, gate_part), not rep_peers)
        for h in range(per):
            dd[h] = ddt[h].T
        for s, j in enumerate(rep_peers):
            rsd_send[group, s] = dd[:, rows_of(j, down_part)].astype(jnp.bfloat16)
            push(
                rsd_send.at[group, s], rsd_recv.at[group, s],
                rs_s.at[group, 1, s], rs_r.at[group, 1, s], rep_dev(j),
            )

    def settle_gate(group):
        gate = gu_m[...] + dgu[:, :, rows_of(rep, gate_part)]
        for s, j in enumerate(rep_peers):
            got = rs_recv.at[group, s]
            remote(got, got, rs_s.at[group, 0, s], rs_r.at[group, 0, s], rep_dev(j)).wait_recv()
            gate = gate + got[...].astype(jnp.float32)
        gu_m[...] = renorm(gu_m[...], gate)

    def settle_down(group):
        down = d_m[...] + dd[:, rows_of(rep, down_part)]
        for s, j in enumerate(rep_peers):
            got = rsd_recv.at[group, s]
            remote(got, got, rs_s.at[group, 1, s], rs_r.at[group, 1, s], rep_dev(j)).wait_recv()
            down = down + got[...].astype(jnp.float32)
        d_m[...] = renorm(d_m[...], down)

    def apply(group):
        stage = group + 1

        def one(source, into):
            for h in range(per):
                query = qbuf[group, source, h]
                a = dot_nt(query, gu_b[stage, 0, h])
                b = dot_nt(query, gu_b[stage, 1, h])
                hid_act = (a * sigmoid(a) * b).astype(jnp.bfloat16)
                into[h] = dot_nt(hid_act, d_b[stage, h]).astype(jnp.bfloat16)

        def out_copy(s):
            return remote(
                o_send.at[group, s], out_ref.at[group, heads_of(mine)],
                o_s.at[group, s], o_r.at[group, s], part_dev(flip(mine, s + 1, parts)),
            )

        def step(i, carry):
            s = parts - 2 - i
            source = flip(mine, s + 1, parts)
            wait_tokens(group, (2,), source, s)
            one(source, o_send.at[group, s])
            out_copy(s).start()
            return carry

        lax.fori_loop(0, parts - 1, step, 0)
        one(mine, out_ref.at[group, heads_of(mine)])
        for s in range(parts - 1):
            pending.append(out_copy(s))

    def finish(group):
        half = width // 2

        def squares(total, source):
            for h in range(per):
                o = out_ref[group, source * per + h].astype(jnp.float32)
                total = total + (o[:, :half] * o[:, :half] + o[:, half:] * o[:, half:])
            return total

        total = squares(jnp.zeros((block, half), jnp.float32), mine)
        for s, j in reversed(list(enumerate(part_peers))):
            got = out_ref.at[group, heads_of(j)]
            remote(got, got, o_s.at[group, s], o_r.at[group, s], part_dev(j)).wait_recv()
            total = squares(total, j)
        row = jnp.sum(total.T, axis=0, keepdims=True)
        ms_send[group] = jnp.broadcast_to(row, ms_send.shape[1:])
        for s, j in enumerate(head_peers):
            push(
                ms_send.at[group], ms_recv.at[group, s],
                ms_s.at[group, s], ms_r.at[group, s], (j, tok),
            )
        for s, j in enumerate(head_peers):
            got = ms_recv.at[group, s]
            remote(got, got, ms_s.at[group, s], ms_r.at[group, s], (j, tok)).wait_recv()
            row = row + got[:1]
        valid = lax.broadcasted_iota(jnp.int32, (1, block), 1) < cnt_ref[group, tok]
        mean = row / (head_n * heads * width)
        scale_ref[pl.ds(group, 1), :] = lax.rsqrt(mean + epsilon) * valid.astype(jnp.float32)

    for s, j in enumerate(part_peers):
        for kind, got in enumerate(owned(0, j)):
            remote(got, got, w_s.at[kind, s], w_r.at[kind, s], part_dev(j)).wait_recv()
    share_gate(0)
    share_down(0)
    if narrow_gate:
        gu_m[...] = gu_b[0, :, :, rows_of(rep, gate_part)].astype(jnp.float32)
    if narrow_down:
        d_m[...] = d_b[0, :, rows_of(rep, down_part)].astype(jnp.float32)
    wait_share(0)
    finals = (fin_g, fin_u, fin_d)
    for group in range(groups):
        def between():
            if group + 1 < groups:
                send_tokens(group + 1, (0, 1))
            if group > 0:
                send_tokens(group, (2,))

        update(group, between)
        if group > 0:
            apply(group - 1)
        settle_gate(group)
        share_gate(group + 1)
        settle_down(group)
        share_down(group + 1)
        if group == 0:
            send_tokens(0, (2,))
        if group + 1 == groups:
            for s, j in enumerate(part_peers):
                for kind, (src, dst) in enumerate(zip(owned(groups, j), finals)):
                    push(src, dst.at[heads_of(mine)], f_s.at[kind, s], f_r.at[kind, s], part_dev(j))
            for src, dst in zip(owned(groups, mine), finals):
                dst[heads_of(mine)] = src[...]
        if group > 0:
            finish(group - 1)
        wait_share(group + 1)
    apply(groups - 1)
    finish(groups - 1)
    for s, j in enumerate(part_peers):
        for kind, dst in enumerate(finals):
            got = dst.at[heads_of(j)]
            remote(got, got, f_s.at[kind, s], f_r.at[kind, s], part_dev(j)).wait_recv()
    fg_ref[...] = fin_g[...].astype(jnp.float32)
    fu_ref[...] = fin_u[...].astype(jnp.float32)
    fd_ref[...] = fin_d[...].astype(jnp.float32)
    for copy in pending:
        copy.wait_send()


def on_device(
    queries, key_vectors, value_vectors, step_rates, counts, out_gain, w_gate, w_up, w_down
):
    tok_n, head_n = lax.axis_size("tok"), lax.axis_size("head")
    groups, heads, block, width = key_vectors.shape
    hidden = w_down.shape[2]
    parts = min(heads, tok_n)
    per, reps = heads // parts, tok_n // parts
    gate_rows, down_rows = w_gate.shape[1], w_down.shape[1]
    gate_part, down_part = parts * gate_rows, parts * down_rows
    grad_scale = float(tok_n * block) ** (-0.5)
    bf16, f32 = jnp.bfloat16, jnp.float32

    def wire(rows):
        return bf16 if rows % 16 == 0 else f32

    vmem, dma = pltpu.VMEM, pltpu.SemaphoreType.DMA
    pn, rn, hn = max(parts - 1, 1), max(reps - 1, 1), max(head_n - 1, 1)
    scratch = [
        vmem(value_vectors.shape, bf16),
        vmem((max(8, heads), block), f32),
        vmem((groups, parts, per, block, width), bf16),
        vmem((groups, parts, per, block, width), bf16),
        vmem((groups, parts, per, block, width), bf16),
        vmem((groups, pn, per, block, width), bf16),
        vmem(w_gate.shape, wire(gate_rows)),
        vmem(w_up.shape, wire(gate_rows)),
        vmem(w_down.shape, wire(down_rows)),
        vmem(w_gate.shape, wire(gate_rows)),
        vmem(w_up.shape, wire(gate_rows)),
        vmem(w_down.shape, wire(down_rows)),
        vmem((2, per, gate_part, width), f32),
        vmem((per, down_part, hidden), f32),
        vmem((groups + 1, 2, per, hidden, width), bf16),
        vmem((groups + 1, per, width, hidden), bf16),
        vmem((per, hidden, width), bf16),
        vmem((2, per, hidden, width), f32),
        vmem((per, hidden, width), f32),
        vmem((per, width, hidden), f32),
        vmem((groups, rn, 2, per, gate_part, width), bf16),
        vmem((groups, rn, 2, per, gate_part, width), bf16),
        vmem((groups, rn, per, down_part, hidden), bf16),
        vmem((groups, rn, per, down_part, hidden), bf16),
        vmem((groups, 8, block), f32),
        vmem((groups, hn, 8, block), f32),
        dma((groups, 3)),
        dma((groups, 3, pn)), dma((groups, 3, pn)),
        dma((3, pn)), dma((3, pn)),
        dma((groups, pn)), dma((groups, pn)),
        dma((3, pn)), dma((3, pn)),
        dma((groups, 2, rn)), dma((groups, 2, rn)),
        dma((groups + 1, 2, rn)), dma((groups + 1, 2, rn)),
        dma((groups, hn)), dma((groups, hn)),
    ]
    whole = pl.BlockSpec(memory_space=pltpu.VMEM)
    hbm = pl.BlockSpec(memory_space=pl.ANY)
    flops = groups * heads * 9 * 2 * block * width * hidden
    produced, scale, final_gate, final_up, final_down = pl.pallas_call(
        functools.partial(kernel, (tok_n, head_n, parts, reps, per, grad_scale)),
        out_shape=(
            jax.ShapeDtypeStruct(queries.shape, bf16),
            jax.ShapeDtypeStruct((groups, block), f32),
            jax.ShapeDtypeStruct(w_gate.shape, f32),
            jax.ShapeDtypeStruct(w_up.shape, f32),
            jax.ShapeDtypeStruct(w_down.shape, f32),
        ),
        in_specs=[pl.BlockSpec(memory_space=pltpu.SMEM), hbm, whole, hbm] + [whole] * 4,
        out_specs=(whole,) * 5,
        scratch_shapes=scratch,
        cost_estimate=pl.CostEstimate(
            flops=flops, bytes_accessed=8 * queries.size, transcendentals=0
        ),
        compiler_params=pltpu.CompilerParams(
            collective_id=0, has_side_effects=True, vmem_limit_bytes=56 * 1024 * 1024
        ),
    )(counts, key_vectors, value_vectors, queries, step_rates, w_gate, w_up, w_down)
    mixed = (
        produced.astype(f32) * out_gain[None, :, None, :] * scale[:, None, :, None]
    ).astype(bf16)
    return mixed, final_gate, final_up, final_down


def solution(mesh):
    tokens = P(None, "head", "tok", None)
    weight = P("head", "tok", None)
    in_specs = (
        tokens, tokens, tokens, P(None, "head", "tok"), P(), P("head", None),
        weight, weight, weight,
    )
    return jax.shard_map(
        on_device, mesh=mesh, in_specs=in_specs,
        out_specs=(tokens, weight, weight, weight), check_vma=False,
    )
```
